32 devices in a mesh: groups: 2 (over y), src: 8 (over z, x), own: 2 (over core).
Axes of the slice: x: 2, y: 2, z: 4, core: 2. Of those that a mesh axis runs over, the one named last changes fastest.
Arguments:
- embeddings: bfloat16 [32768, 768], P(('groups', 'src', 'own')), parts along dimension 0, may hold values from -100 to 100
- cluster_id: int32 [32768], P(('groups', 'src', 'own')), parts along dimension 0, may hold values from 0 to 31, as said below
- member_rank: int32 [32768], P(('groups', 'src', 'own')), parts along dimension 0, may hold values from 0 to 1023, as said below
Outputs:
- best_similarity: float32 [32768], P(('groups', 'src', 'own')), parts along dimension 0
The draws below stay inside these ranges and needn't reach their ends.
There are 2 independent parts, one for each index of `groups`. The reference program is written for one: setup_inputs(seed, part) draws one part's arguments, and reference() takes and returns one part's arrays. A program takes and returns all parts, laid end to end along the dimension named above; each array names one. Nothing has to cross between parts.
Inputs may be any that keep to these rules, and one draw needn't show every extreme that they name: `cluster_id`: cluster c is owned by device c mod 16 of the group (src major, own minor). Every device holds exactly 64 rows of the clusters of each owner. Cluster sizes are uneven: in every draw the rows of some owner all belong to one of its clusters. `member_rank`: the rows of one cluster carry the ranks 0 to its size - 1, each once. A cluster has at most 1024 rows, and in every draw one cluster has exactly that many.
All inputs are finite; a program needn't handle non-finite values.
Results may differ from the reference program's by a relative error of at most 0.0009.
Values may be sent and summed in bfloat16 or wider, within the bound.
A program may use at most 64 MiB of HBM per device.

```python
import math
import jax
import jax.numpy as jnp
from jax import lax

D = 768
ROWS_DEV = 1024
CL_DEV = 2
OWNERS = 16
SLOT = 64
ROWS = 16384


def layout(key):
    hot_key, pick_key, member_key = jax.random.split(key, 3)
    hot_owner = jax.random.randint(hot_key, (), 0, OWNERS)
    base = (jnp.arange(ROWS_DEV, dtype=jnp.int32) // SLOT).astype(jnp.int32)

    def one_source(subkey):
        return jax.random.permutation(subkey, base).astype(jnp.int32)
    owners_of_rows = jax.vmap(one_source)(jax.random.split(pick_key, OWNERS)).reshape(ROWS)
    member = jax.random.randint(member_key, (ROWS,), 0, CL_DEV)
    member = jnp.where(owners_of_rows == hot_owner, 0, member)
    return (owners_of_rows + OWNERS * member).astype(jnp.int32)


def ordering(key):
    clusters = layout(key)
    order_key = jax.random.fold_in(key, 2)
    priority = jax.random.permutation(order_key, ROWS).astype(jnp.int32)
    sort_key = clusters * ROWS + priority
    row_order = jnp.argsort(sort_key).astype(jnp.int32)
    sorted_clusters = clusters[row_order]
    first = jnp.searchsorted(sorted_clusters, sorted_clusters, side='left').astype(jnp.int32)
    rank_sorted = jnp.arange(ROWS, dtype=jnp.int32) - first
    return (clusters, row_order, rank_sorted)


def draw_cluster_id(key, part):
    return layout(key)


def draw_member_rank(key, part):
    clusters, row_order, rank_sorted = ordering(key)
    return jnp.zeros((ROWS,), jnp.int32).at[row_order].set(rank_sorted)


def draw_embeddings(key, part):
    clusters, row_order, rank_sorted = ordering(key)
    key = jax.random.fold_in(key, 3)
    centre_key, spread_key, noise_key, flag_key, copy_key = jax.random.split(key, 5)
    centre = jnp.clip(jax.random.normal(centre_key, (OWNERS, D), jnp.float32), -3.0, 3.0)
    spread = jnp.exp(jax.random.uniform(spread_key, (ROWS, 1), jnp.float32, math.log(0.5), math.log(2.0)))
    flagged = (jax.random.randint(flag_key, (ROWS,), 0, 8) == 0) & (rank_sorted >= 1)
    copied = flagged & jnp.logical_not(jnp.roll(flagged, 1))
    anchor = jnp.roll(copied, -1)
    is_copy = jnp.zeros((ROWS,), jnp.bool_).at[row_order].set(copied)
    is_anchor = jnp.zeros((ROWS,), jnp.bool_).at[row_order].set(anchor)
    parent = jnp.zeros((ROWS,), jnp.int32).at[row_order].set(jnp.roll(row_order, 1))
    spread = jnp.where(is_anchor[:, None], 2.0, spread)
    noise = jnp.clip(jax.random.normal(noise_key, (ROWS, D), jnp.float32), -3.0, 3.0)
    base = centre[clusters % OWNERS] + spread * noise
    copy_noise = jnp.clip(jax.random.normal(copy_key, (ROWS, D), jnp.float32), -3.0, 3.0)
    rows = jnp.where(is_copy[:, None], base[parent] + 0.05 * copy_noise, base)
    return rows.astype(jnp.bfloat16)


def setup_inputs(seed: int = 0, part: int = 0) -> dict:
    key_of = jax.random.split(jax.random.key(seed), 4)
    part_splits = jax.random.split(jax.random.fold_in(key_of[3], part), 4)
    return {
        "embeddings": draw_embeddings(jax.random.fold_in(jax.random.fold_in(key_of[3], part), 71), part),
        "cluster_id": draw_cluster_id(jax.random.fold_in(jax.random.fold_in(key_of[3], part), 71), part),
        "member_rank": draw_member_rank(jax.random.fold_in(jax.random.fold_in(key_of[3], part), 71), part),
    }


EPS = 1e-06

def reference(embeddings, cluster_id, member_rank):
    values = embeddings.astype(jnp.float32)
    normalized = (values / jnp.sqrt(lax.optimization_barrier(jnp.sum(values * values, axis=1, keepdims=True)) + EPS)).astype(jnp.bfloat16)
    owner = (cluster_id % OWNERS).astype(jnp.int32)
    row_order = jnp.argsort(owner, stable=True).astype(jnp.int32)
    sorted_owner = owner[row_order]
    starts = jnp.searchsorted(sorted_owner, jnp.arange(OWNERS, dtype=jnp.int32)).astype(jnp.int32)
    capacity = OWNERS * SLOT
    sorted_rows = jnp.concatenate([normalized[row_order], jnp.zeros((capacity, D), jnp.bfloat16)], axis=0)
    sorted_ids = jnp.concatenate([cluster_id[row_order], jnp.full((capacity,), -1, jnp.int32)], axis=0)
    sorted_rank = jnp.concatenate([member_rank[row_order], jnp.full((capacity,), -1, jnp.int32)], axis=0)

    def one_owner(start):
        rows_here = lax.dynamic_slice_in_dim(sorted_rows, start, capacity, 0)
        ids_here = lax.dynamic_slice_in_dim(sorted_ids, start, capacity, 0)
        rank_here = lax.dynamic_slice_in_dim(sorted_rank, start, capacity, 0)
        similar = jnp.dot(rows_here, rows_here.T, preferred_element_type=jnp.float32)
        earlier = (ids_here[:, None] == ids_here[None, :]) & (rank_here[None, :] < rank_here[:, None])
        return lax.optimization_barrier(jnp.max(jnp.where(earlier, similar, -1.0), axis=1))
    largest = lax.map(one_owner, starts)
    position = jnp.arange(ROWS, dtype=jnp.int32) - starts[sorted_owner]
    picked = largest[sorted_owner, position]
    return jnp.zeros((ROWS,), picked.dtype).at[row_order].set(picked)
```

```python
import functools

import jax
import jax.numpy as jnp
from jax import lax
from jax.experimental import pallas as pl
from jax.experimental.pallas import tpu as pltpu
from jax.sharding import PartitionSpec as P

EPS = 1e-06
MESH = pl.DeviceIdType.MESH
GROUP = 256
GAP = 4096.0
SELF = 1


def log2(n):
    assert n & (n - 1) == 0
    return n.bit_length() - 1


def kernel(
    n_src, n_own, slot, emb_hbm, cid_ref, rank_ref, out_ref,
    emb, stage, recv, mstage, mrecv, rstage, rrecv, keyrow, baserow, keycol, best,
    in_sem, d_send, d_recv, m_send, m_recv, r_send, r_recv,
):
    n = n_src * n_own
    h = n_src // 2
    rows, width = emb.shape
    chunks = rows // 128
    per_group = GROUP // slot
    groups = n // per_group
    s = lax.axis_index("src")
    c = lax.axis_index("own")
    half, off = s // h, s % h

    def place(t, sign):
        near, q = t % 2, t // 2
        j, cc = q // n_own, q % n_own
        side = half if near else 1 - half
        return {
            "src": side * h + (off + h + sign * j) % h,
            "own": (c + n_own + sign * cc) % n_own,
        }

    others = [t for t in range(n) if t != SELF]
    load = pltpu.make_async_copy(emb_hbm, emb, in_sem)
    load.start()
    barrier = pltpu.get_barrier_semaphore()
    for t in others:
        pl.semaphore_signal(barrier, inc=1, device_id=place(t, 1), device_id_type=MESH)

    cid = cid_ref[...]
    owner = cid & (n - 1)
    ds, dc = owner >> log2(n_own), owner & (n_own - 1)
    near = jnp.where((ds >> log2(h)) == half, 1, 0)
    step = 2 * ((((ds & (h - 1)) - off) & (h - 1)) * n_own + ((dc - c) & (n_own - 1))) + near
    upper = jnp.where(
        lax.broadcasted_iota(jnp.int32, (128, 128), 0) < lax.broadcasted_iota(jnp.int32, (128, 128), 1),
        1.0, 0.0,
    ).astype(jnp.bfloat16)
    which = lax.broadcasted_iota(jnp.int32, (n, 128), 0)
    hot = [jnp.where(which == step[k : k + 1, :], 1.0, 0.0) for k in range(chunks)]
    within = jnp.dot(
        jnp.concatenate(hot, axis=0).astype(jnp.bfloat16), upper, preferred_element_type=jnp.float32
    )
    seen = jnp.zeros((n, 1), jnp.float32)
    pos = []
    for k in range(chunks):
        pos.append(jnp.sum(hot[k] * (within[k * n : (k + 1) * n] + seen), axis=0, keepdims=True))
        seen = seen + jnp.sum(hot[k], axis=1, keepdims=True)
    pos = jnp.concatenate(pos, axis=1).astype(jnp.int32)

    def as_row(x):
        return jnp.concatenate([x[k : k + 1, :] for k in range(chunks)], axis=1)

    step_row = as_row(step)
    target = step_row * slot + pos
    rank = rank_ref[...]
    meta = jnp.concatenate(
        [as_row((cid >> log2(n)) + 1), as_row(rank >> 5), as_row(rank & 31), jnp.zeros((5, rows), jnp.int32)],
        axis=0,
    ).astype(jnp.float32).astype(jnp.bfloat16)
    mstage[...] = jnp.zeros_like(mstage)
    mrecv[SELF] = jnp.zeros_like(mrecv[SELF])

    def data_copy(t):
        part = pl.ds(t * slot, slot)
        return pltpu.make_async_remote_copy(
            src_ref=stage.at[part], dst_ref=recv.at[part], send_sem=d_send.at[t], recv_sem=d_recv.at[t],
            device_id=place(t, 1), device_id_type=MESH,
        )

    def meta_copy(t):
        return pltpu.make_async_remote_copy(
            src_ref=mstage.at[t], dst_ref=mrecv.at[t], send_sem=m_send.at[t], recv_sem=m_recv.at[t],
            device_id=place(t, 1), device_id_type=MESH,
        )

    def result_copy(t):
        return pltpu.make_async_remote_copy(
            src_ref=rstage.at[t], dst_ref=rrecv.at[t], send_sem=r_send.at[t], recv_sem=r_recv.at[t],
            device_id=place(t, -1), device_id_type=MESH,
        )

    load.wait()
    for g in range(groups):
        slots = lax.broadcasted_iota(jnp.int32, (GROUP, rows), 0) + g * GROUP
        pick = jnp.where(slots == target, 1.0, 0.0).astype(jnp.bfloat16)
        picked = jnp.dot(pick, emb[...], preferred_element_type=jnp.float32)
        scale = 1.0 / jnp.sqrt(jnp.sum(picked * picked, axis=1, keepdims=True) + EPS)
        normalized = (picked * scale).astype(jnp.bfloat16)
        stage[pl.ds(g * GROUP, GROUP), :] = normalized
        about = lax.dot_general(
            meta, pick, (((1,), (1,)), ((), ())), preferred_element_type=jnp.float32
        )
        about = jnp.concatenate([about[0:1], about[1:2] * 32.0 + about[2:3]], axis=0)
        for u in range(per_group):
            t = g * per_group + u
            piece = about[:, u * slot : (u + 1) * slot]
            if t == SELF:
                recv[pl.ds(t * slot, slot), :] = normalized[u * slot : (u + 1) * slot]
                mrecv[t, :, 0:slot] = piece
            else:
                mstage[t, :, 0:slot] = piece
        if g == 0:
            pl.semaphore_wait(barrier, n - 1)
        for u in range(per_group):
            t = g * per_group + u
            if t != SELF:
                meta_copy(t).start()
                data_copy(t).start()

    best[...] = jnp.full_like(best, -1.0)

    def score(k, q):
        similar = lax.dot_general(
            recv[pl.ds(k * GROUP, GROUP), :], recv[pl.ds(q * GROUP, GROUP), :],
            (((1,), (1,)), ((), ())), preferred_element_type=jnp.float32,
        )
        key = keycol[k]
        key = jnp.concatenate([key] * (GROUP // 128), axis=1)
        earlier = (key < keyrow[q]) & (key >= baserow[q])
        best[q] = jnp.maximum(
            best[q], jnp.max(jnp.where(earlier, similar, -1.0), axis=0, keepdims=True)
        )

    for g in range(groups):
        pieces = []
        for u in range(per_group):
            t = g * per_group + u
            if t != SELF:
                meta_copy(t).wait_recv()
            pieces.append(mrecv[t, :, 0:slot])
        pieces = jnp.concatenate(pieces, axis=1)
        base = pieces[0:1] * GAP
        key = base + pieces[1:2]
        baserow[g] = base
        keyrow[g] = key
        keycol[g] = jnp.broadcast_to(key, (128, GROUP)).T
        for u in range(per_group):
            t = g * per_group + u
            if t != SELF:
                data_copy(t).wait_recv()
        for k in range(g):
            score(g, k)
            score(k, g)
        score(g, g)

    rstage[...] = jnp.zeros_like(rstage)
    rrecv[SELF] = jnp.zeros_like(rrecv[SELF])
    for g in range(groups):
        value = best[g]
        for u in range(per_group):
            t = g * per_group + u
            piece = value[:, u * slot : (u + 1) * slot]
            if t == SELF:
                rrecv[t, :, 0:slot] = piece
            else:
                rstage[t, :, 0:slot] = piece
                result_copy(t).start()

    hot_pos = jnp.where(
        lax.broadcasted_iota(jnp.int32, (128, rows), 0) == pos, 1.0, 0.0
    ).astype(jnp.bfloat16)
    hot_step = lax.broadcasted_iota(jnp.int32, (n, rows), 0) == step_row
    for t in others:
        result_copy(t).wait_recv()
    back = rrecv[:, 0, :]
    high = back.astype(jnp.bfloat16)
    rest = back - high.astype(jnp.float32)
    mid = rest.astype(jnp.bfloat16)
    low = (rest - mid.astype(jnp.float32)).astype(jnp.bfloat16)
    spread = jnp.dot(
        jnp.concatenate([high, mid, low], axis=0), hot_pos, preferred_element_type=jnp.float32
    )
    spread = (spread[0:n] + spread[n : 2 * n]) + spread[2 * n :]
    result = jnp.sum(jnp.where(hot_step, spread, 0.0), axis=0, keepdims=True)
    for k in range(chunks):
        out_ref[k : k + 1, :] = result[:, k * 128 : (k + 1) * 128]
    for t in others:
        meta_copy(t).wait_send()
        data_copy(t).wait_send()
        result_copy(t).wait_send()


def shards(embeddings, cluster_id, member_rank):
    rows, width = embeddings.shape
    n_src = lax.axis_size("src")
    n_own = lax.axis_size("own")
    n = n_src * n_own
    slot = -(-(rows // n) // 16) * 16
    groups = n * slot // GROUP
    f32, bf16 = jnp.float32, jnp.bfloat16
    out = pl.pallas_call(
        functools.partial(kernel, n_src, n_own, slot),
        out_shape=jax.ShapeDtypeStruct((rows // 128, 128), f32),
        in_specs=[
            pl.BlockSpec(memory_space=pl.ANY),
            pl.BlockSpec(memory_space=pltpu.VMEM),
            pl.BlockSpec(memory_space=pltpu.VMEM),
        ],
        out_specs=pl.BlockSpec(memory_space=pltpu.VMEM),
        scratch_shapes=[
            pltpu.VMEM((rows, width), bf16),
            pltpu.VMEM((n * slot, width), bf16),
            pltpu.VMEM((n * slot, width), bf16),
            pltpu.VMEM((n, 2, 128), f32),
            pltpu.VMEM((n, 2, 128), f32),
            pltpu.VMEM((n, 1, 128), f32),
            pltpu.VMEM((n, 1, 128), f32),
            pltpu.VMEM((groups, 1, GROUP), f32),
            pltpu.VMEM((groups, 1, GROUP), f32),
            pltpu.VMEM((groups, GROUP, 128), f32),
            pltpu.VMEM((groups, 1, GROUP), f32),
            pltpu.SemaphoreType.DMA,
        ]
        + [pltpu.SemaphoreType.DMA((n,))] * 6,
        compiler_params=pltpu.CompilerParams(
            collective_id=0, has_side_effects=True, vmem_limit_bytes=40 * 1024 * 1024
        ),
    )(embeddings, cluster_id.reshape(rows // 128, 128), member_rank.reshape(rows // 128, 128))
    return out.reshape(rows)


def solution(mesh):
    in_specs = (
        P(("groups", "src", "own"), None),
        P(("groups", "src", "own")),
        P(("groups", "src", "own")),
    )
    out_specs = P(("groups", "src", "own"))
    return jax.shard_map(shards, mesh=mesh, in_specs=in_specs, out_specs=out_specs, check_vma=False)
```

```python
import functools

import jax
import jax.numpy as jnp
from jax import lax
from jax.experimental import pallas as pl
from jax.experimental.pallas import tpu as pltpu
from jax.sharding import PartitionSpec as P

EPS = 1e-06
MESH = pl.DeviceIdType.MESH
GROUP = 256
GAP = 4096.0


def plan(h, n_own):
    return [(near, j, c) for j in range(h) for c in range(n_own) for near in (0, 1)]


def log2(n):
    assert n & (n - 1) == 0
    return n.bit_length() - 1


def kernel(
    n_src, n_own, slot, emb_hbm, cid_hbm, rank_hbm, out_ref,
    emb, cid_ref, rank_ref, stage, recv, mstage, mrecv, rstage, rrecv, keyrow, baserow, keycol, best,
    in_sems, d_send, d_recv, m_send, m_recv, r_send, r_recv,
):
    n = n_src * n_own
    h = n_src // 2
    rows, width = emb.shape
    chunks = rows // 128
    per_group = GROUP // slot
    groups = n // per_group
    s = lax.axis_index("src")
    c = lax.axis_index("own")
    half, off = s // h, s % h

    def place(t, sign):
        near, j, cc = order[t]
        side = half if near else 1 - half
        return {
            "src": side * h + (off + h + sign * j) % h,
            "own": (c + n_own + sign * cc) % n_own,
        }

    order = plan(h, n_own)
    SELF = order.index((1, 0, 0))
    others = [t for t in range(n) if t != SELF]
    loads = [
        pltpu.make_async_copy(src, dst, in_sems.at[i])
        for i, (src, dst) in enumerate([(cid_hbm, cid_ref), (rank_hbm, rank_ref), (emb_hbm, emb)])
    ]
    for load in loads:
        load.start()
    barrier = pltpu.get_barrier_semaphore()
    for t in others:
        pl.semaphore_signal(barrier, inc=1, device_id=place(t, 1), device_id_type=MESH)

    loads[0].wait()
    loads[1].wait()
    cid = cid_ref[...]
    owner = cid & (n - 1)
    ds, dc = owner >> log2(n_own), owner & (n_own - 1)
    near = jnp.where((ds >> log2(h)) == half, 1, 0)
    code = (near * h + ((ds - off) & (h - 1))) * n_own + ((dc - c) & (n_own - 1))
    step = jnp.zeros_like(code)
    for t, (near, j, cc) in enumerate(order):
        step = jnp.where(code == (near * h + j) * n_own + cc, t, step)
    upper = jnp.where(
        lax.broadcasted_iota(jnp.int32, (128, 128), 0) < lax.broadcasted_iota(jnp.int32, (128, 128), 1),
        1.0, 0.0,
    ).astype(jnp.bfloat16)
    which = lax.broadcasted_iota(jnp.int32, (n, 128), 0)
    hot = [jnp.where(which == step[k : k + 1, :], 1.0, 0.0) for k in range(chunks)]
    within = jnp.dot(
        jnp.concatenate(hot, axis=0).astype(jnp.bfloat16), upper, preferred_element_type=jnp.float32
    )
    seen = jnp.zeros((n, 1), jnp.float32)
    pos = []
    for k in range(chunks):
        pos.append(jnp.sum(hot[k] * (within[k * n : (k + 1) * n] + seen), axis=0, keepdims=True))
        seen = seen + jnp.sum(hot[k], axis=1, keepdims=True)
    pos = jnp.concatenate(pos, axis=1).astype(jnp.int32)

    def as_row(x):
        return jnp.concatenate([x[k : k + 1, :] for k in range(chunks)], axis=1)

    step_row = as_row(step)
    target = step_row * slot + pos
    rank = rank_ref[...]
    meta = jnp.concatenate(
        [as_row((cid >> log2(n)) + 1), as_row(rank >> 5), as_row(rank & 31), jnp.zeros((5, rows), jnp.int32)],
        axis=0,
    ).astype(jnp.float32).astype(jnp.bfloat16)
    mstage[...] = jnp.zeros_like(mstage)
    mrecv[SELF] = jnp.zeros_like(mrecv[SELF])

    def data_copy(t):
        part = pl.ds(t * slot, slot)
        return pltpu.make_async_remote_copy(
            src_ref=stage.at[part], dst_ref=recv.at[part], send_sem=d_send.at[t], recv_sem=d_recv.at[t],
            device_id=place(t, 1), device_id_type=MESH,
        )

    def meta_copy(t):
        return pltpu.make_async_remote_copy(
            src_ref=mstage.at[t], dst_ref=mrecv.at[t], send_sem=m_send.at[t], recv_sem=m_recv.at[t],
            device_id=place(t, 1), device_id_type=MESH,
        )

    def result_copy(t):
        return pltpu.make_async_remote_copy(
            src_ref=rstage.at[t], dst_ref=rrecv.at[t], send_sem=r_send.at[t], recv_sem=r_recv.at[t],
            device_id=place(t, -1), device_id_type=MESH,
        )

    loads[2].wait()
    for g in range(groups):
        slots = lax.broadcasted_iota(jnp.int32, (GROUP, rows), 0) + g * GROUP
        pick = jnp.where(slots == target, 1.0, 0.0).astype(jnp.bfloat16)
        picked = jnp.dot(pick, emb[...], preferred_element_type=jnp.float32)
        scale = 1.0 / jnp.sqrt(jnp.sum(picked * picked, axis=1, keepdims=True) + EPS)
        normalized = (picked * scale).astype(jnp.bfloat16)
        stage[pl.ds(g * GROUP, GROUP), :] = normalized
        about = lax.dot_general(
            meta, pick, (((1,), (1,)), ((), ())), preferred_element_type=jnp.float32
        )
        about = jnp.concatenate([about[0:1], about[1:2] * 32.0 + about[2:3]], axis=0)
        for u in range(per_group):
            t = g * per_group + u
            piece = about[:, u * slot : (u + 1) * slot]
            if t == SELF:
                recv[pl.ds(t * slot, slot), :] = normalized[u * slot : (u + 1) * slot]
                mrecv[t, :, 0:slot] = piece
            else:
                mstage[t, :, 0:slot] = piece
        if g == 0:
            pl.semaphore_wait(barrier, n - 1)
        for u in range(per_group):
            t = g * per_group + u
            if t != SELF:
                meta_copy(t).start()
                data_copy(t).start()

    best[...] = jnp.full_like(best, -1.0)

    def score(k, q):
        similar = lax.dot_general(
            recv[pl.ds(k * GROUP, GROUP), :], recv[pl.ds(q * GROUP, GROUP), :],
            (((1,), (1,)), ((), ())), preferred_element_type=jnp.float32,
        )
        key = keycol[k]
        key = jnp.concatenate([key] * (GROUP // 128), axis=1)
        earlier = (key < keyrow[q]) & (key >= baserow[q])
        best[q] = jnp.maximum(
            best[q], jnp.max(jnp.where(earlier, similar, -1.0), axis=0, keepdims=True)
        )

    for g in range(groups):
        pieces = []
        for u in range(per_group):
            t = g * per_group + u
            if t != SELF:
                meta_copy(t).wait_recv()
            pieces.append(mrecv[t, :, 0:slot])
        pieces = jnp.concatenate(pieces, axis=1)
        base = pieces[0:1] * GAP
        key = base + pieces[1:2]
        baserow[g] = base
        keyrow[g] = key
        keycol[g] = jnp.broadcast_to(key, (128, GROUP)).T
        for u in range(per_group):
            t = g * per_group + u
            if t != SELF:
                data_copy(t).wait_recv()
        for k in range(g):
            score(g, k)
            score(k, g)
        score(g, g)

    rstage[...] = jnp.zeros_like(rstage)
    rrecv[SELF] = jnp.zeros_like(rrecv[SELF])
    for g in range(groups):
        value = best[g]
        for u in range(per_group):
            t = g * per_group + u
            piece = value[:, u * slot : (u + 1) * slot]
            if t == SELF:
                rrecv[t, :, 0:slot] = piece
            else:
                rstage[t, :, 0:slot] = piece
                result_copy(t).start()

    hot_pos = jnp.where(
        lax.broadcasted_iota(jnp.int32, (128, rows), 0) == pos, 1.0, 0.0
    ).astype(jnp.bfloat16)
    hot_step = lax.broadcasted_iota(jnp.int32, (n, rows), 0) == step_row
    for t in others:
        result_copy(t).wait_recv()
    back = rrecv[:, 0, :]
    high = back.astype(jnp.bfloat16)
    rest = back - high.astype(jnp.float32)
    mid = rest.astype(jnp.bfloat16)
    low = (rest - mid.astype(jnp.float32)).astype(jnp.bfloat16)
    spread = jnp.dot(
        jnp.concatenate([high, mid, low], axis=0), hot_pos, preferred_element_type=jnp.float32
    )
    spread = (spread[0:n] + spread[n : 2 * n]) + spread[2 * n :]
    result = jnp.sum(jnp.where(hot_step, spread, 0.0), axis=0, keepdims=True)
    for k in range(chunks):
        out_ref[k : k + 1, :] = result[:, k * 128 : (k + 1) * 128]
    for t in others:
        meta_copy(t).wait_send()
        data_copy(t).wait_send()
        result_copy(t).wait_send()


def shards(embeddings, cluster_id, member_rank):
    rows, width = embeddings.shape
    n_src = lax.axis_size("src")
    n_own = lax.axis_size("own")
    n = n_src * n_own
    slot = -(-(rows // n) // 16) * 16
    groups = n * slot // GROUP
    f32, bf16 = jnp.float32, jnp.bfloat16
    out = pl.pallas_call(
        functools.partial(kernel, n_src, n_own, slot),
        out_shape=jax.ShapeDtypeStruct((rows // 128, 128), f32),
        in_specs=[
            pl.BlockSpec(memory_space=pltpu.HBM),
            pl.BlockSpec(memory_space=pltpu.HBM),
            pl.BlockSpec(memory_space=pltpu.HBM),
        ],
        out_specs=pl.BlockSpec(memory_space=pltpu.VMEM),
        scratch_shapes=[
            pltpu.VMEM((rows, width), bf16),
            pltpu.VMEM((rows // 128, 128), jnp.int32),
            pltpu.VMEM((rows // 128, 128), jnp.int32),
            pltpu.VMEM((n * slot, width), bf16),
            pltpu.VMEM((n * slot, width), bf16),
            pltpu.VMEM((n, 2, 128), f32),
            pltpu.VMEM((n, 2, 128), f32),
            pltpu.VMEM((n, 1, 128), f32),
            pltpu.VMEM((n, 1, 128), f32),
            pltpu.VMEM((groups, 1, GROUP), f32),
            pltpu.VMEM((groups, 1, GROUP), f32),
            pltpu.VMEM((groups, GROUP, 128), f32),
            pltpu.VMEM((groups, 1, GROUP), f32),
            pltpu.SemaphoreType.DMA((3,)),
        ]
        + [pltpu.SemaphoreType.DMA((n,))] * 6,
        compiler_params=pltpu.CompilerParams(
            collective_id=0, has_side_effects=True, vmem_limit_bytes=60 * 1024 * 1024
        ),
    )(embeddings, cluster_id.reshape(rows // 128, 128), member_rank.reshape(rows // 128, 128))
    return out.reshape(rows)


def solution(mesh):
    in_specs = (
        P(("groups", "src", "own"), None),
        P(("groups", "src", "own")),
        P(("groups", "src", "own")),
    )
    out_specs = P(("groups", "src", "own"))
    return jax.shard_map(shards, mesh=mesh, in_specs=in_specs, out_specs=out_specs, check_vma=False)
```

```python
import functools

import jax
import jax.numpy as jnp
from jax import lax
from jax.experimental import pallas as pl
from jax.experimental.pallas import tpu as pltpu
from jax.sharding import PartitionSpec as P

EPS = 1e-06
MESH = pl.DeviceIdType.MESH
GROUP = 256
GAP = 4096.0


def plan(h, n_own):
    return [(near, j, c) for j in range(h) for c in range(n_own) for near in (0, 1)]


def log2(n):
    assert n & (n - 1) == 0
    return n.bit_length() - 1


def kernel(
    n_src, n_own, slot, emb_hbm, cid_hbm, rank_hbm, out_ref,
    emb, cid_ref, rank_ref, stage, recv, mstage, mrecv, rstage, rrecv, keyrow, baserow, keycol, best,
    in_sems, d_send, d_recv, m_send, m_recv, r_send, r_recv,
):
    n = n_src * n_own
    h = n_src // 2
    rows, width = emb.shape
    chunks = rows // 128
    per_group = GROUP // slot
    groups = n // per_group
    s = lax.axis_index("src")
    c = lax.axis_index("own")
    half, off = s // h, s % h

    def place(t, sign):
        near, j, cc = order[t]
        side = half if near else 1 - half
        return {
            "src": side * h + (off + h + sign * j) % h,
            "own": (c + n_own + sign * cc) % n_own,
        }

    order = plan(h, n_own)
    SELF = order.index((1, 0, 0))
    others = [t for t in range(n) if t != SELF]
    loads = [
        pltpu.make_async_copy(src, dst, in_sems.at[i])
        for i, (src, dst) in enumerate([(cid_hbm, cid_ref), (rank_hbm, rank_ref), (emb_hbm, emb)])
    ]
    for load in loads:
        load.start()
    barrier = pltpu.get_barrier_semaphore()
    for t in others:
        pl.semaphore_signal(barrier, inc=1, device_id=place(t, 1), device_id_type=MESH)

    loads[0].wait()
    loads[1].wait()
    cid = cid_ref[...]
    owner = cid & (n - 1)
    ds, dc = owner >> log2(n_own), owner & (n_own - 1)
    near = jnp.where((ds >> log2(h)) == half, 1, 0)
    code = (near * h + ((ds - off) & (h - 1))) * n_own + ((dc - c) & (n_own - 1))
    step = jnp.zeros_like(code)
    for t, (near, j, cc) in enumerate(order):
        step = jnp.where(code == (near * h + j) * n_own + cc, t, step)
    upper = jnp.where(
        lax.broadcasted_iota(jnp.int32, (128, 128), 0) < lax.broadcasted_iota(jnp.int32, (128, 128), 1),
        1.0, 0.0,
    ).astype(jnp.bfloat16)
    which = lax.broadcasted_iota(jnp.int32, (n, 128), 0)
    hot = [jnp.where(which == step[k : k + 1, :], 1.0, 0.0) for k in range(chunks)]
    within = jnp.dot(
        jnp.concatenate(hot, axis=0).astype(jnp.bfloat16), upper, preferred_element_type=jnp.float32
    )
    seen = jnp.zeros((n, 1), jnp.float32)
    pos = []
    for k in range(chunks):
        pos.append(jnp.sum(hot[k] * (within[k * n : (k + 1) * n] + seen), axis=0, keepdims=True))
        seen = seen + jnp.sum(hot[k], axis=1, keepdims=True)
    pos = jnp.concatenate(pos, axis=1).astype(jnp.int32)

    def as_row(x):
        return jnp.concatenate([x[k : k + 1, :] for k in range(chunks)], axis=1)

    step_row = as_row(step)
    target = step_row * slot + pos
    rank = rank_ref[...]
    meta = jnp.concatenate(
        [as_row((cid >> log2(n)) + 1), as_row(rank >> 5), as_row(rank & 31), jnp.zeros((5, rows), jnp.int32)],
        axis=0,
    ).astype(jnp.float32).astype(jnp.bfloat16)
    mstage[...] = jnp.zeros_like(mstage)
    mrecv[SELF] = jnp.zeros_like(mrecv[SELF])

    def data_copy(t):
        part = pl.ds(t * slot, slot)
        return pltpu.make_async_remote_copy(
            src_ref=stage.at[part], dst_ref=recv.at[part], send_sem=d_send.at[t], recv_sem=d_recv.at[t],
            device_id=place(t, 1), device_id_type=MESH,
        )

    def meta_copy(t):
        return pltpu.make_async_remote_copy(
            src_ref=mstage.at[t], dst_ref=mrecv.at[t], send_sem=m_send.at[t], recv_sem=m_recv.at[t],
            device_id=place(t, 1), device_id_type=MESH,
        )

    def result_copy(t):
        return pltpu.make_async_remote_copy(
            src_ref=rstage.at[t], dst_ref=rrecv.at[t], send_sem=r_send.at[t], recv_sem=r_recv.at[t],
            device_id=place(t, -1), device_id_type=MESH,
        )

    loads[2].wait()
    for g in range(groups):
        slots = lax.broadcasted_iota(jnp.int32, (GROUP, rows), 0) + g * GROUP
        pick = jnp.where(slots == target, 1.0, 0.0).astype(jnp.bfloat16)
        picked = jnp.dot(pick, emb[...], preferred_element_type=jnp.float32)
        scale = 1.0 / jnp.sqrt(jnp.sum(picked * picked, axis=1, keepdims=True) + EPS)
        normalized = (picked * scale).astype(jnp.bfloat16)
        stage[pl.ds(g * GROUP, GROUP), :] = normalized
        about = lax.dot_general(
            meta, pick, (((1,), (1,)), ((), ())), preferred_element_type=jnp.float32
        )
        about = jnp.concatenate([about[0:1], about[1:2] * 32.0 + about[2:3]], axis=0)
        for u in range(per_group):
            t = g * per_group + u
            piece = about[:, u * slot : (u + 1) * slot]
            if t == SELF:
                recv[pl.ds(t * slot, slot), :] = normalized[u * slot : (u + 1) * slot]
                mrecv[t, :, 0:slot] = piece
            else:
                mstage[t, :, 0:slot] = piece
        if g == 0:
            pl.semaphore_wait(barrier, n - 1)
        for u in range(per_group):
            t = g * per_group + u
            if t != SELF:
                meta_copy(t).start()
                data_copy(t).start()

    best[...] = jnp.full_like(best, -1.0)

    def score(k, q):
        similar = lax.dot_general(
            recv[pl.ds(k * GROUP, GROUP), :], recv[pl.ds(q * GROUP, GROUP), :],
            (((1,), (1,)), ((), ())), preferred_element_type=jnp.float32,
        )
        key = keycol[k]
        key = jnp.concatenate([key] * (GROUP // 128), axis=1)
        earlier = (key < keyrow[q]) & (key >= baserow[q])
        best[q] = jnp.maximum(
            best[q], jnp.max(jnp.where(earlier, similar, -1.0), axis=0, keepdims=True)
        )

    for g in range(groups):
        pieces = []
        for u in range(per_group):
            t = g * per_group + u
            if t != SELF:
                meta_copy(t).wait_recv()
            pieces.append(mrecv[t, :, 0:slot])
        pieces = jnp.concatenate(pieces, axis=1)
        base = pieces[0:1] * GAP
        key = base + pieces[1:2]
        baserow[g] = base
        keyrow[g] = key
        keycol[g] = jnp.broadcast_to(key, (128, GROUP)).T
        for u in range(per_group):
            t = g * per_group + u
            if t != SELF:
                data_copy(t).wait_recv()
        for k in range(g):
            score(g, k)
            score(k, g)
        score(g, g)

    rstage[...] = jnp.zeros_like(rstage)
    rrecv[SELF] = jnp.zeros_like(rrecv[SELF])
    for g in range(groups):
        value = best[g]
        for u in range(per_group):
            t = g * per_group + u
            piece = value[:, u * slot : (u + 1) * slot]
            if t == SELF:
                rrecv[t, :, 0:slot] = piece
            else:
                rstage[t, :, 0:slot] = piece
                result_copy(t).start()

    hot_pos = jnp.where(
        lax.broadcasted_iota(jnp.int32, (128, rows), 0) == pos, 1.0, 0.0
    ).astype(jnp.bfloat16)
    hot_step = lax.broadcasted_iota(jnp.int32, (n, rows), 0) == step_row
    for t in others:
        result_copy(t).wait_recv()
    back = rrecv[:, 0, :]
    high = back.astype(jnp.bfloat16)
    rest = back - high.astype(jnp.float32)
    mid = rest.astype(jnp.bfloat16)
    low = (rest - mid.astype(jnp.float32)).astype(jnp.bfloat16)
    spread = jnp.dot(
        jnp.concatenate([high, mid, low], axis=0), hot_pos, preferred_element_type=jnp.float32
    )
    spread = (spread[0:n] + spread[n : 2 * n]) + spread[2 * n :]
    result = jnp.sum(jnp.where(hot_step, spread, 0.0), axis=0, keepdims=True)
    for k in range(chunks):
        out_ref[k : k + 1, :] = result[:, k * 128 : (k + 1) * 128]
    for t in others:
        meta_copy(t).wait_send()
        data_copy(t).wait_send()
        result_copy(t).wait_send()


def shards(embeddings, cluster_id, member_rank):
    rows, width = embeddings.shape
    n_src = lax.axis_size("src")
    n_own = lax.axis_size("own")
    n = n_src * n_own
    slot = -(-(rows // n) // 16) * 16
    groups = n * slot // GROUP
    f32, bf16 = jnp.float32, jnp.bfloat16
    out = pl.pallas_call(
        functools.partial(kernel, n_src, n_own, slot),
        out_shape=pltpu.VMEM((rows // 128, 128), f32),
        in_specs=[
            pl.BlockSpec(memory_space=pltpu.HBM),
            pl.BlockSpec(memory_space=pltpu.HBM),
            pl.BlockSpec(memory_space=pltpu.HBM),
        ],
        out_specs=pl.BlockSpec(memory_space=pltpu.VMEM),
        scratch_shapes=[
            pltpu.VMEM((rows, width), bf16),
            pltpu.VMEM((rows // 128, 128), jnp.int32),
            pltpu.VMEM((rows // 128, 128), jnp.int32),
            pltpu.VMEM((n * slot, width), bf16),
            pltpu.VMEM((n * slot, width), bf16),
            pltpu.VMEM((n, 2, 128), f32),
            pltpu.VMEM((n, 2, 128), f32),
            pltpu.VMEM((n, 1, 128), f32),
            pltpu.VMEM((n, 1, 128), f32),
            pltpu.VMEM((groups, 1, GROUP), f32),
            pltpu.VMEM((groups, 1, GROUP), f32),
            pltpu.VMEM((groups, GROUP, 128), f32),
            pltpu.VMEM((groups, 1, GROUP), f32),
            pltpu.SemaphoreType.DMA((3,)),
        ]
        + [pltpu.SemaphoreType.DMA((n,))] * 6,
        compiler_params=pltpu.CompilerParams(
            collective_id=0, has_side_effects=True, vmem_limit_bytes=60 * 1024 * 1024
        ),
    )(embeddings, cluster_id.reshape(rows // 128, 128), member_rank.reshape(rows // 128, 128))
    return out.reshape(rows)


def solution(mesh):
    in_specs = (
        P(("groups", "src", "own"), None),
        P(("groups", "src", "own")),
        P(("groups", "src", "own")),
    )
    out_specs = P(("groups", "src", "own"))
    return jax.shard_map(shards, mesh=mesh, in_specs=in_specs, out_specs=out_specs, check_vma=False)
```

```python
import functools

import jax
import jax.numpy as jnp
from jax import lax
from jax.experimental import pallas as pl
from jax.experimental.pallas import tpu as pltpu
from jax.sharding import PartitionSpec as P

EPS = 1e-06
MESH = pl.DeviceIdType.MESH
GROUP = 256
GAP = 4096.0


def plan(h, n_own):
    return [(near, j, c) for j in range(h) for c in range(n_own) for near in (1, 0)]


def log2(n):
    assert n & (n - 1) == 0
    return n.bit_length() - 1


def kernel(
    n_src, n_own, slot, emb_hbm, cid_hbm, rank_hbm, out_ref,
    emb, cid_ref, rank_ref, stage, recv, mstage, mrecv, rstage, rrecv, keyrow, baserow, keycol, best, hot_pos, hot_step,
    in_sems, d_send, d_recv, m_send, m_recv, r_send, r_recv,
):
    n = n_src * n_own
    h = n_src // 2
    rows, width = emb.shape
    chunks = rows // 128
    per_group = GROUP // slot
    groups = n // per_group
    s = lax.axis_index("src")
    c = lax.axis_index("own")
    half, off = s // h, s % h

    def place(t, sign):
        near, j, cc = order[t]
        side = half if near else 1 - half
        return {
            "src": side * h + (off + h + sign * j) % h,
            "own": (c + n_own + sign * cc) % n_own,
        }

    order = plan(h, n_own)
    SELF = 0
    others = range(1, n)
    to = [place(t, 1) for t in range(n)]
    back_to = [place(t, -1) for t in range(n)]
    loads = [
        pltpu.make_async_copy(src, dst, in_sems.at[i])
        for i, (src, dst) in enumerate([(cid_hbm, cid_ref), (rank_hbm, rank_ref), (emb_hbm, emb)])
    ]
    for load in loads:
        load.start()
    barrier = pltpu.get_barrier_semaphore()
    for t in others:
        pl.semaphore_signal(barrier, inc=1, device_id=to[t], device_id_type=MESH)

    loads[0].wait()
    loads[1].wait()
    cid = cid_ref[...]
    owner = cid & (n - 1)
    ds, dc = owner >> log2(n_own), owner & (n_own - 1)
    near = jnp.where((ds >> log2(h)) == half, 1, 0)
    code = (near * h + ((ds - off) & (h - 1))) * n_own + ((dc - c) & (n_own - 1))
    step = jnp.zeros_like(code)
    for t, (near, j, cc) in enumerate(order):
        step = jnp.where(code == (near * h + j) * n_own + cc, t, step)
    upper = jnp.where(
        lax.broadcasted_iota(jnp.int32, (128, 128), 0) < lax.broadcasted_iota(jnp.int32, (128, 128), 1),
        1.0, 0.0,
    ).astype(jnp.bfloat16)
    which = lax.broadcasted_iota(jnp.int32, (n, 128), 0)
    hot = [jnp.where(which == step[k : k + 1, :], 1.0, 0.0) for k in range(chunks)]
    within = jnp.dot(
        jnp.concatenate(hot, axis=0).astype(jnp.bfloat16), upper, preferred_element_type=jnp.float32
    )
    seen = jnp.zeros((n, 1), jnp.float32)
    pos = []
    for k in range(chunks):
        pos.append(jnp.sum(hot[k] * (within[k * n : (k + 1) * n] + seen), axis=0, keepdims=True))
        seen = seen + jnp.sum(hot[k], axis=1, keepdims=True)
    pos = jnp.concatenate(pos, axis=1).astype(jnp.int32)

    def as_row(x):
        return jnp.concatenate([x[k : k + 1, :] for k in range(chunks)], axis=1)

    step_row = as_row(step)
    target = step_row * slot + pos
    rank = rank_ref[...]
    meta = jnp.concatenate(
        [as_row((cid >> log2(n)) + 1), as_row(rank >> 5), as_row(rank & 31), jnp.zeros((5, rows), jnp.int32)],
        axis=0,
    ).astype(jnp.float32).astype(jnp.bfloat16)
    mstage[...] = jnp.zeros_like(mstage)
    mrecv[SELF] = jnp.zeros_like(mrecv[SELF])

    def data_copy(t):
        part = pl.ds(t * slot, slot)
        return pltpu.make_async_remote_copy(
            src_ref=stage.at[part], dst_ref=recv.at[part], send_sem=d_send.at[t // per_group], recv_sem=d_recv.at[t // per_group],
            device_id=to[t], device_id_type=MESH,
        )

    def meta_copy(t):
        return pltpu.make_async_remote_copy(
            src_ref=mstage.at[t], dst_ref=mrecv.at[t], send_sem=m_send, recv_sem=m_recv.at[t // per_group],
            device_id=to[t], device_id_type=MESH,
        )

    def result_copy(t):
        return pltpu.make_async_remote_copy(
            src_ref=rstage.at[t], dst_ref=rrecv.at[t], send_sem=r_send, recv_sem=r_recv,
            device_id=back_to[t], device_id_type=MESH,
        )

    def settle(ref, first, count, sem):
        part = ref.at[pl.ds(first, count)]
        pltpu.make_async_copy(part, part, sem).wait()

    def span(g):
        first = max(g * per_group, 1)
        return first, (g + 1) * per_group - first

    loads[2].wait()
    for g in range(groups):
        slots = lax.broadcasted_iota(jnp.int32, (GROUP, rows), 0) + g * GROUP
        pick = jnp.where(slots == target, 1.0, 0.0).astype(jnp.bfloat16)
        picked = jnp.dot(pick, emb[...], preferred_element_type=jnp.float32)
        scale = 1.0 / jnp.sqrt(jnp.sum(picked * picked, axis=1, keepdims=True) + EPS)
        normalized = (picked * scale).astype(jnp.bfloat16)
        stage[pl.ds(g * GROUP, GROUP), :] = normalized
        about = lax.dot_general(
            meta, pick, (((1,), (1,)), ((), ())), preferred_element_type=jnp.float32
        )
        about = jnp.concatenate([about[0:1], about[1:2] * 32.0 + about[2:3]], axis=0)
        for u in range(per_group):
            t = g * per_group + u
            piece = about[:, u * slot : (u + 1) * slot]
            if t == SELF:
                recv[pl.ds(t * slot, slot), :] = normalized[u * slot : (u + 1) * slot]
                mrecv[t, :, 0:slot] = piece
            else:
                mstage[t, :, 0:slot] = piece
        if g == 0:
            pl.semaphore_wait(barrier, n - 1)
        for u in range(per_group):
            t = g * per_group + u
            if t != SELF:
                meta_copy(t).start()
                data_copy(t).start()

    hot_pos[...] = jnp.where(
        lax.broadcasted_iota(jnp.int32, (128, rows), 0) == pos, 1.0, 0.0
    ).astype(jnp.bfloat16)
    hot_step[...] = jnp.where(
        lax.broadcasted_iota(jnp.int32, (n, rows), 0) == step_row, 1.0, 0.0
    )
    rstage[...] = jnp.zeros_like(rstage)
    rrecv[SELF] = jnp.zeros_like(rrecv[SELF])
    best[...] = jnp.full_like(best, -1.0)

    def score(k, q):
        similar = lax.dot_general(
            recv[pl.ds(k * GROUP, GROUP), :], recv[pl.ds(q * GROUP, GROUP), :],
            (((1,), (1,)), ((), ())), preferred_element_type=jnp.float32,
        )
        key = keycol[k]
        key = jnp.concatenate([key] * (GROUP // 128), axis=1)
        earlier = (key < keyrow[q]) & (key >= baserow[q])
        best[q] = jnp.maximum(
            best[q], jnp.max(jnp.where(earlier, similar, -1.0), axis=0, keepdims=True)
        )

    for g in range(groups):
        first, count = span(g)
        settle(mrecv, first, count, m_recv.at[g])
        pieces = []
        for u in range(per_group):
            t = g * per_group + u
            pieces.append(mrecv[t, :, 0:slot])
        pieces = jnp.concatenate(pieces, axis=1)
        base = pieces[0:1] * GAP
        key = base + pieces[1:2]
        baserow[g] = base
        keyrow[g] = key
        keycol[g] = jnp.broadcast_to(key, (128, GROUP)).T
        if g == groups - 1:
            settle(mstage, 1, n - 1, m_send)
            for k in range(g):
                settle(stage, span(k)[0] * slot, span(k)[1] * slot, d_send.at[k])
        settle(recv, first * slot, count * slot, d_recv.at[g])
        for k in range(g):
            score(g, k)
            score(k, g)
        score(g, g)

    for g in range(groups):
        value = best[g]
        for u in range(per_group):
            t = g * per_group + u
            piece = value[:, u * slot : (u + 1) * slot]
            if t == SELF:
                rrecv[t, :, 0:slot] = piece
            else:
                rstage[t, :, 0:slot] = piece
    for t in others:
        result_copy(t).start()
    settle(stage, span(groups - 1)[0] * slot, span(groups - 1)[1] * slot, d_send.at[groups - 1])
    settle(rstage, 1, n - 1, r_send)
    settle(rrecv, 1, n - 1, r_recv)
    back = rrecv[:, 0, :]
    high = back.astype(jnp.bfloat16)
    rest = back - high.astype(jnp.float32)
    mid = rest.astype(jnp.bfloat16)
    low = (rest - mid.astype(jnp.float32)).astype(jnp.bfloat16)
    spread = jnp.dot(
        jnp.concatenate([high, mid, low], axis=0), hot_pos[...], preferred_element_type=jnp.float32
    )
    spread = (spread[0:n] + spread[n : 2 * n]) + spread[2 * n :]
    result = jnp.sum(hot_step[...] * spread, axis=0, keepdims=True)
    for k in range(chunks):
        out_ref[k : k + 1, :] = result[:, k * 128 : (k + 1) * 128]


def shards(embeddings, cluster_id, member_rank):
    rows, width = embeddings.shape
    n_src = lax.axis_size("src")
    n_own = lax.axis_size("own")
    n = n_src * n_own
    slot = -(-(rows // n) // 16) * 16
    groups = n * slot // GROUP
    f32, bf16 = jnp.float32, jnp.bfloat16
    out = pl.pallas_call(
        functools.partial(kernel, n_src, n_own, slot),
        out_shape=pltpu.VMEM((rows // 128, 128), f32),
        in_specs=[
            pl.BlockSpec(memory_space=pltpu.HBM),
            pl.BlockSpec(memory_space=pltpu.HBM),
            pl.BlockSpec(memory_space=pltpu.HBM),
        ],
        out_specs=pl.BlockSpec(memory_space=pltpu.VMEM),
        scratch_shapes=[
            pltpu.VMEM((rows, width), bf16),
            pltpu.VMEM((rows // 128, 128), jnp.int32),
            pltpu.VMEM((rows // 128, 128), jnp.int32),
            pltpu.VMEM((n * slot, width), bf16),
            pltpu.VMEM((n * slot, width), bf16),
            pltpu.VMEM((n, 2, 128), f32),
            pltpu.VMEM((n, 2, 128), f32),
            pltpu.VMEM((n, 1, 128), f32),
            pltpu.VMEM((n, 1, 128), f32),
            pltpu.VMEM((groups, 1, GROUP), f32),
            pltpu.VMEM((groups, 1, GROUP), f32),
            pltpu.VMEM((groups, GROUP, 128), f32),
            pltpu.VMEM((groups, 1, GROUP), f32),
            pltpu.VMEM((128, rows), bf16),
            pltpu.VMEM((n, rows), f32),
            pltpu.SemaphoreType.DMA((3,)),
            pltpu.SemaphoreType.DMA((groups,)),
            pltpu.SemaphoreType.DMA((groups,)),
            pltpu.SemaphoreType.DMA,
            pltpu.SemaphoreType.DMA((groups,)),
            pltpu.SemaphoreType.DMA,
            pltpu.SemaphoreType.DMA,
        ],
        compiler_params=pltpu.CompilerParams(
            collective_id=0, has_side_effects=True, vmem_limit_bytes=60 * 1024 * 1024
        ),
    )(embeddings, cluster_id.reshape(rows // 128, 128), member_rank.reshape(rows // 128, 128))
    return out.reshape(rows)


def solution(mesh):
    in_specs = (
        P(("groups", "src", "own"), None),
        P(("groups", "src", "own")),
        P(("groups", "src", "own")),
    )
    out_specs = P(("groups", "src", "own"))
    return jax.shard_map(shards, mesh=mesh, in_specs=in_specs, out_specs=out_specs, check_vma=False)
```
